32 devices in a mesh: wide: 8 (over z, x), narrow: 4 (over y, core).
Axes of the slice: x: 2, y: 2, z: 4, core: 2. Of those that a mesh axis runs over, the one named last changes fastest.
Arguments:
- embeddings: bfloat16 [16384, 768], P(('wide', 'narrow')), may hold values from -6 to 6
- coarse_ids: int32 [16384, 1], P(('wide', 'narrow')), may hold values from 0 to 7; in each aligned block of 512 rows (0 to 511, 512 to 1023, ...) at most 128 rows name the same one
- fine_ids: int32 [16384], P(('wide', 'narrow')), may hold values from 0 to 2047
- centroids: bfloat16 [16384, 768], P(('wide', 'narrow')), may hold values from -6 to 6
- candidates: int32 [128, 8], P(('wide', 'narrow')), may hold values from 0 to 63, as said below
Outputs:
- new_centroids: bfloat16 [16384, 768], P(('wide', 'narrow'))
- best_score: float32 [16384], P(('wide', 'narrow'))
The draws below stay inside these ranges and needn't reach their ends.
Inputs may be any that keep to these rules, and one draw needn't show every extreme that they name: `candidates`: counting the 32 entries of the 4 consecutive query blocks of one device, at most 8 lie among the 8 blocks of one coarse cluster, and some coarse cluster holds exactly 8 of every device's entries.
All inputs are finite; a program needn't handle non-finite values.
Results may differ from the reference program's by a relative error of at most 0.0055.
Values may be sent and summed in bfloat16 or wider, within the bound.
A program may use at most 192 MiB of HBM per device.

```python
import math
import jax
import jax.numpy as jnp
import numpy as np
from jax import lax

D = 768
QROWS = 128
CBLK = 256
K_CAND = 8
EMB_DEV = 512
COARSE = 8
CGROUP = 2048
BLK_GROUP = 8
CENTS = 16384
NBLK = 64
EMBS = 16384
QB = 4
NQB = 128
REQS = 32
CAP = 8
ACAP = 128


def draw_candidates(key, part):
    key_hot, key_dev = jax.random.split(key)
    device_count = NQB // QB
    hot_group = jax.random.randint(key_hot, (), 0, COARSE)

    def per_device(index):
        dev_key = jax.random.fold_in(key_dev, index)
        key_first, key_second, key_third = jax.random.split(dev_key, 3)
        spread = jax.random.permutation(key_first, (COARSE - 1) * CAP)[:REQS - CAP]
        others = spread // CAP
        others = others + (others >= hot_group).astype(jnp.int32)
        groups = jnp.concatenate([jnp.full((CAP,), hot_group, jnp.int32), others.astype(jnp.int32)])
        groups = jax.random.permutation(key_second, groups)
        within = jax.random.randint(key_third, (REQS,), 0, BLK_GROUP)
        return (groups * BLK_GROUP + within).astype(jnp.int32)
    flat = jax.vmap(per_device)(jnp.arange(device_count))
    return flat.reshape(NQB, K_CAND).astype(jnp.int32)


def set_ends(result, rng, least, largest):
    place = [jax.random.randint(jax.random.fold_in(rng, axis), (), 0, length) for axis, length in enumerate(result.shape)]
    longest = result.shape.index(max(result.shape))
    neighbour = place[:longest] + [(place[longest] + 1) % result.shape[longest]] + place[longest + 1:]
    return result.at[tuple(place)].set(least).at[tuple(neighbour)].set(largest)


def block_scale(rng, shape, cuts, least, largest):
    level = 1.0
    for position, parts in cuts:
        steps = jax.random.uniform(jax.random.fold_in(jax.random.fold_in(rng, 6), position), (parts,), jnp.float32, least / len(cuts), largest / len(cuts))
        level = level * jnp.repeat(jnp.exp(steps), shape[position] // parts).reshape((-1,) + (1,) * (len(shape) - 1 - position))
    return level


def deal_out(stream_key, own, number, rows, count, top, limit, slope):
    ranking = jax.random.permutation(stream_key, count)
    heavy_load, usual = portions_of(count, rows * top, limit, slope, True), portions_of(count, rows * top, limit, slope, False)
    places = jnp.arange(count)

    def named(sizes, rotation):
        used = int((sizes > 0).sum())
        fixed = max(1, used // 4)
        moved = fixed + (places - fixed + rotation * (used - fixed)) % max(1, count - fixed)
        return jnp.zeros((count,), jnp.int32).at[ranking[jnp.where(places < fixed, places, moved)]].set(jnp.asarray(sizes, jnp.int32))

    sizes = jnp.where(number % 4 == 0, named(heavy_load, number // 4), named(usual, number - number // 4 - 1))
    mixed = jax.random.permutation(jax.random.fold_in(own, 3), count)
    donor, sink = mixed[0:count // 2 * 2:2], mixed[1:count // 2 * 2:2]
    room = jnp.minimum(sizes[donor] - 1, limit - sizes[sink]) // 2
    room = jnp.where((donor == ranking[0]) | (sink == ranking[0]) | (sizes[sink] == 0), 0, jnp.maximum(room, 0))
    moved = jax.random.randint(jax.random.fold_in(own, 4), (count // 2,), 0, 1 << 20) % (room + 1)
    sizes = sizes.at[donor].add(-moved).at[sink].add(moved)
    items = jnp.searchsorted(jnp.cumsum(sizes), jnp.arange(rows * top), side="right").astype(jnp.int32)
    grid = items.reshape(top, rows).T
    grid = grid[jax.random.permutation(jax.random.fold_in(own, 1), rows)]
    rotation = jax.random.randint(jax.random.fold_in(own, 2), (rows, 1), 0, top)
    return jnp.take_along_axis(grid, (jnp.arange(top)[None, :] + rotation) % top, axis=1)


def portions_of(amount, total, bound, lean, full):
    portions = [(1 << 20) // math.isqrt(standing ** lean) + 1 for standing in range(1, amount + 1)]
    largest = bound if full else min(bound, max(-(-total // amount), total * portions[0] // sum(portions)))
    least = 1 if total - largest >= amount - 1 else 0
    counts, rest = [largest] + [least] * (amount - 1), total - largest - least * (amount - 1)
    while rest > 0:
        movable = [i for i in range(1, amount) if counts[i] < largest] or [i for i in range(1, amount) if counts[i] < bound]
        whole, left = sum([portions[i] for i in movable]), rest
        for i in movable:
            more = min(bound - counts[i], max(1, left * portions[i] // whole), rest)
            counts[i] = counts[i] + more
            rest = rest - more
    return np.array(counts)


def bell_draw(own_key, dims, deviation, bound, shards=(), held_as=jnp.bfloat16):
    array = jax.random.normal(own_key, dims, jnp.float32) * deviation
    if len(shards) > 0:
        array = block_scale(own_key, dims, shards, -0.22, 0.18) * array
    return jnp.clip(array, min=-bound, max=bound).astype(held_as)


def setup_inputs(seed: int = 0) -> dict:
    splits = jax.random.split(jax.random.key(seed), 6)
    embeddings = bell_draw(splits[0], (EMBS, D), 1.0, 6.0, ((0, 32),))
    coarse_ids_keys = jax.random.split(jax.random.fold_in(splits[1], 1), EMBS // EMB_DEV)
    coarse_ids_turns = jax.random.permutation(jax.random.fold_in(splits[1], 3), EMBS // EMB_DEV)
    coarse_ids = jax.vmap(lambda own, number: deal_out(jax.random.fold_in(splits[1], 2), own, number, EMB_DEV, COARSE, 1, ACAP, 2))(coarse_ids_keys, coarse_ids_turns).reshape((EMBS, 1))
    fine_ids = set_ends(jax.random.randint(splits[2], (EMBS,), 0, CGROUP), jax.random.fold_in(splits[2], 1), 0, CGROUP - 1).astype(jnp.int32)
    centroids = bell_draw(splits[3], (CENTS, D), 1.0, 6.0, ((0, 32),))
    candidates = draw_candidates(jax.random.fold_in(splits[5], 71), 0)
    return {"embeddings": embeddings, "coarse_ids": coarse_ids, "fine_ids": fine_ids, "centroids": centroids, "candidates": candidates}


def reference(embeddings, coarse_ids, fine_ids, centroids, candidates):
    assign = (coarse_ids[:, 0] * CGROUP + fine_ids).astype(jnp.int32)
    sums = jax.ops.segment_sum(embeddings.astype(jnp.float32), assign, num_segments=CENTS)
    mixed = centroids.astype(jnp.float32) + sums
    scale_row = lax.rsqrt(lax.optimization_barrier(jnp.mean(mixed * mixed, axis=1, keepdims=True)) + 1e-06)
    new_centroids = (mixed * scale_row).astype(jnp.bfloat16)
    blocks = new_centroids.reshape(NBLK, CBLK, D)
    query_blocks = embeddings.reshape(NQB, QROWS, D)

    def one_block(operands):
        query, picks = operands
        chosen = jnp.take(blocks, picks, axis=0).astype(jnp.float32)
        scores = jnp.einsum('nd,kcd->nkc', query.astype(jnp.float32), chosen)
        return lax.optimization_barrier(jnp.max(scores, axis=(1, 2))) * D ** (-0.5)
    best_score = lax.map(one_block, (query_blocks, candidates)).reshape(EMBS)
    return (new_centroids, best_score)
```

```python
import functools

import jax
import jax.numpy as jnp
from jax import lax
from jax.experimental import pallas as pl
from jax.experimental.pallas import tpu as pltpu
from jax.sharding import PartitionSpec as P

QROWS = 128
CBLK = 256
K_CAND = 8
WORD = 32
MESH = pl.DeviceIdType.MESH


def refine_kernel(
    emb_ref, meta_ref, cent_ref, newc_ref, best_ref,
    emb_all, meta_all, cent_all, acc, psend, precv, newc, part, part_in,
    send_sem, recv_sem, meta_send, meta_recv, cent_sem, psum_send, psum_recv, part_send, part_recv,
):
    rows, width = emb_ref.shape
    half = rows // 2
    peers = emb_all.shape[0]
    chip_cents = cent_all.shape[0]
    tiles = chip_cents // CBLK
    wide = lax.axis_index("wide")
    narrow = lax.axis_index("narrow")
    z, x = wide // 2, wide % 2
    y, core = narrow // 2, narrow % 2
    me = wide * 2 + y
    low = z < 2
    inner = jnp.logical_or(z == 1, z == 2)
    outer = jnp.logical_not(inner)
    partner = z + 1 - 2 * (z % 2)
    across = 3 - z
    levels = (z, partner, jnp.where(low, 2, 1), jnp.where(low, 3, 0))

    def slot(column, k):
        xx = 1 - x if column in "XD" else x
        yy = 1 - y if column in "YD" else y
        return (levels[k] * 2 + xx) * 2 + yy

    slots = {c + str(k): slot(c, k) for c in "OXYD" for k in range(4)}

    def device(zz, xx, yy):
        return (zz * 2 + xx, yy * 2 + core)

    links = {
        "x": (0, device(z, 1 - x, y)),
        "y": (1, device(z, x, 1 - y)),
        "pair": (2, device(partner, x, y)),
        "cross": (3, device(across, x, y)),
    }
    twin = (wide, y * 2 + 1 - core)

    def peer(j):
        return (j // 2, (j % 2) * 2 + core)

    def chunk(link, j, h):
        number, target = links[link]
        piece = emb_all.at[j, pl.ds(h * half, half), :]
        return pltpu.make_async_remote_copy(
            src_ref=piece, dst_ref=piece, send_sem=send_sem.at[number, j, h],
            recv_sem=recv_sem.at[j, h], device_id=target, device_id_type=MESH,
        )

    sent = []

    def forward(name, h, *names):
        j = slots[name]
        for link in names:
            sent.append((link, j, h))
            if link == "cross":
                pl.when(inner)(lambda: chunk("cross", j, h).start())
            else:
                chunk(link, j, h).start()

    def forward_inner(name, h, link):
        j = slots[name]
        sent.append(("inner_" + link, j, h))
        chunk(link, j, h).start()

    def arrive(name, h):
        chunk("x", slots[name], h).wait_recv()

    barrier = pltpu.get_barrier_semaphore()

    @pl.loop(1, peers)
    def _(k):
        pl.semaphore_signal(barrier, inc=1, device_id=peer((me + k) % peers), device_id_type=MESH)

    pl.semaphore_signal(barrier, inc=1, device_id=twin, device_id_type=MESH)
    emb_all[me] = emb_ref[...]
    meta_all[me] = meta_ref[...]
    cent_all[pl.ds(pl.multiple_of(core * rows, rows), rows), :] = cent_ref[...]
    pl.semaphore_wait(barrier, peers)

    def meta_copy(target, source):
        return pltpu.make_async_remote_copy(
            src_ref=meta_ref, dst_ref=meta_all.at[source], send_sem=meta_send.at[target],
            recv_sem=meta_recv.at[source], device_id=peer(target), device_id_type=MESH,
        )

    def own_cents():
        return cent_all.at[pl.ds(pl.multiple_of(core * rows, rows), rows), :]

    cent_copy = pltpu.make_async_remote_copy(
        src_ref=own_cents(), dst_ref=own_cents(), send_sem=cent_sem.at[0],
        recv_sem=cent_sem.at[1], device_id=twin, device_id_type=MESH,
    )

    base = (wide * 4 + y * 2) * rows
    order = ("O0", "O1", "X0", "Y0", "X1", "Y1", "O2", "D0", "O3", "D1", "X2", "Y2", "D2", "X3", "Y3", "D3")

    def at_0():
        @pl.loop(1, peers)
        def _(k):
            meta_copy((me + k) % peers, me).start()

        for h in (0, 1):
            forward("O0", h, "pair", "cross", "x")
            forward("O0", 1 - h, "y")
        cent_copy.start()

        @pl.loop(1, peers)
        def _(k):
            j = (me + k) % peers
            meta_copy(j, j).wait_recv()

    def at_1():
        for h in (0, 1):
            arrive("O1", h)
            forward("O1", h, "cross", "x")
            if h == 1:
                forward("O1", 1, "y")
                forward("O1", 0, "y")

    def corner(k):
        def go():
            arrive(f"X{k}", 0)
            forward(f"X{k}", 0, "y")
            arrive(f"Y{k}", 1)
            forward(f"Y{k}", 1, "x")
            arrive(f"X{k}", 1)
            arrive(f"Y{k}", 0)

        return go

    def inner_to_pair(name):
        def go():
            @pl.when(inner)
            def _():
                for h in (0, 1):
                    arrive(name, h)
                    forward_inner(name, h, "pair")

        return go

    def outer_arrive(name):
        @pl.when(outer)
        def _():
            for h in (0, 1):
                arrive(name, h)

    def to_plane(name):
        def go():
            outer_arrive(name)
            for h in (0, 1):
                forward(name, h, "x")
                forward(name, 1 - h, "y")

        return go

    def to_cross(name):
        def go():
            for h in (0, 1):
                arrive(name, h)
                forward(name, h, "cross")

        return go

    def both(name):
        def go():
            for h in (0, 1):
                arrive(name, h)

        return go

    def at_10():
        inner_to_pair("D2")()
        both("X2")()

    def at_12():
        outer_arrive("D2")
        inner_to_pair("D3")()

    steps = (
        at_0, at_1, corner(0), inner_to_pair("O2"), corner(1), inner_to_pair("O3"),
        to_plane("O2"), to_cross("D0"), to_plane("O3"), to_cross("D1"),
        at_10, both("Y2"), at_12, both("X3"), both("Y3"), lambda: outer_arrive("D3"),
    )

    acc[...] = jnp.zeros_like(acc)

    @pl.loop(0, len(order))
    def _(i):
        j = jnp.int32(0)
        for n, step in enumerate(steps):
            pl.when(i == n)(step)
            j = j + jnp.where(i == n, slots[order[n]], 0)
        ids = meta_all[j][:, :rows] - base
        for t in range(tiles):
            spot = lax.broadcasted_iota(jnp.int32, (CBLK, rows), 0) + t * CBLK
            hot = jnp.where(spot == ids, 1.0, 0.0).astype(jnp.bfloat16)
            acc[t * CBLK : (t + 1) * CBLK, :] += jnp.dot(
                hot, emb_all[j], preferred_element_type=jnp.float32
            )

    def psum_copy(t):
        return pltpu.make_async_remote_copy(
            src_ref=psend.at[t], dst_ref=precv.at[t], send_sem=psum_send.at[t],
            recv_sem=psum_recv.at[t], device_id=twin, device_id_type=MESH,
        )

    for t in range(tiles):
        psend[t] = acc[t * CBLK : (t + 1) * CBLK, :].astype(jnp.bfloat16)
        psum_copy(t).start()
    cent_copy.wait()
    for t in range(tiles):
        psum_copy(t).wait()
        mixed = cent_all[t * CBLK : (t + 1) * CBLK, :].astype(jnp.float32) + (
            psend[t].astype(jnp.float32) + precv[t].astype(jnp.float32)
        )
        scale = lax.rsqrt(jnp.mean(mixed * mixed, axis=1, keepdims=True) + 1e-06)
        newc[t * CBLK : (t + 1) * CBLK, :] = (mixed * scale).astype(jnp.bfloat16)

    def part_copy(target, source):
        return pltpu.make_async_remote_copy(
            src_ref=part.at[target], dst_ref=part_in.at[source], send_sem=part_send.at[target],
            recv_sem=part_recv.at[source], device_id=peer(target), device_id_type=MESH,
        )

    first = (wide * 4 + y * 2) * (rows // CBLK)
    word, shift = first // WORD, first % WORD

    @pl.loop(1, peers + 1)
    def _(k):
        j = (me + k) % peers
        words = meta_all[j]
        bits = jnp.where(word == 0, words[:, rows : 2 * rows], words[:, 2 * rows : 3 * rows])
        best = jnp.full((1, rows), -jnp.inf, jnp.float32)
        for t in range(tiles):
            scores = lax.dot_general(
                newc[t * CBLK : (t + 1) * CBLK, :], emb_all[j], (((1,), (1,)), ((), ())),
                preferred_element_type=jnp.float32,
            )
            top = jnp.max(scores, axis=0, keepdims=True)
            live = jnp.bitwise_and(jnp.right_shift(bits, shift + t), 1) == 1
            best = jnp.maximum(best, jnp.where(live, top, -jnp.inf))
        part[j] = best

        @pl.when(k < peers)
        def _():
            part_copy(j, me).start()

    newc_ref[...] = newc[pl.ds(pl.multiple_of(core * rows, rows), rows), :]

    @pl.loop(1, peers)
    def _(k):
        j = (me + k) % peers
        part_copy(j, j).wait_recv()

    part_in[me] = part[me]
    best = part_in[0]
    for j in range(1, peers):
        best = jnp.maximum(best, part_in[j])
    best_ref[...] = best * width ** (-0.5)

    for link, j, h in sent:
        if link.startswith("inner_"):
            pl.when(inner)(lambda: chunk(link[6:], j, h).wait_send())
        elif link == "cross":
            pl.when(inner)(lambda: chunk(link, j, h).wait_send())
        else:
            chunk(link, j, h).wait_send()

    @pl.loop(1, peers)
    def _(k):
        j = (me + k) % peers
        meta_copy(j, me).wait_send()
        part_copy(j, me).wait_send()


def gathered_step(embeddings, coarse_ids, fine_ids, centroids, candidates):
    rows, width = embeddings.shape
    narrow_count = lax.axis_size("narrow")
    peers = lax.axis_size("wide") * narrow_count // 2
    assign = coarse_ids[:, 0] * (centroids.shape[0] * narrow_count) + fine_ids
    words = []
    for w in range(2):
        flags = jnp.where(
            candidates // WORD == w, jnp.left_shift(jnp.int32(1), candidates % WORD), 0
        )
        mask = flags[:, 0]
        for k in range(1, K_CAND):
            mask = jnp.bitwise_or(mask, flags[:, k])
        words.append(jnp.broadcast_to(mask[:, None], (mask.shape[0], QROWS)).reshape(rows))
    meta = jnp.concatenate([assign, *words]).reshape(1, 3 * rows)
    chip_cents = 2 * centroids.shape[0]
    tiles = chip_cents // CBLK
    new_centroids, best = pl.pallas_call(
        refine_kernel,
        out_shape=(
            jax.ShapeDtypeStruct(centroids.shape, jnp.bfloat16),
            jax.ShapeDtypeStruct((1, rows), jnp.float32),
        ),
        in_specs=[pl.BlockSpec(memory_space=pltpu.VMEM)] * 3,
        out_specs=(pl.BlockSpec(memory_space=pltpu.VMEM),) * 2,
        scratch_shapes=[
            pltpu.VMEM((peers, rows, width), jnp.bfloat16),
            pltpu.VMEM((peers, 1, 3 * rows), jnp.int32),
            pltpu.VMEM((chip_cents, width), jnp.bfloat16),
            pltpu.VMEM((chip_cents, width), jnp.float32),
            pltpu.VMEM((tiles, CBLK, width), jnp.bfloat16),
            pltpu.VMEM((tiles, CBLK, width), jnp.bfloat16),
            pltpu.VMEM((chip_cents, width), jnp.bfloat16),
            pltpu.VMEM((peers, 1, rows), jnp.float32),
            pltpu.VMEM((peers, 1, rows), jnp.float32),
            pltpu.SemaphoreType.DMA((4, peers, 2)),
            pltpu.SemaphoreType.DMA((peers, 2)),
            pltpu.SemaphoreType.DMA((peers,)),
            pltpu.SemaphoreType.DMA((peers,)),
            pltpu.SemaphoreType.DMA((2,)),
            pltpu.SemaphoreType.DMA((tiles,)),
            pltpu.SemaphoreType.DMA((tiles,)),
            pltpu.SemaphoreType.DMA((peers,)),
            pltpu.SemaphoreType.DMA((peers,)),
        ],
        compiler_params=pltpu.CompilerParams(
            collective_id=0, has_side_effects=True, vmem_limit_bytes=48 * 2**20
        ),
    )(embeddings, meta, centroids)
    return new_centroids, best.reshape(rows)


def slot_ranks(targets):
    place = jnp.arange(targets.shape[0], dtype=jnp.int32)
    same = targets[:, None] == targets[None, :]
    return jnp.sum((same & (place[None, :] < place[:, None])).astype(jnp.int32), axis=1)


def pick(table, index):
    return lax.map(lambda i: lax.dynamic_index_in_dim(table, i, keepdims=False), index)


def block_maxima(queries, blocks):
    def one(operands):
        query, block = operands
        scores = jnp.einsum("nd,cd->nc", query, block, preferred_element_type=jnp.float32)
        return jnp.max(scores, axis=1)

    return lax.map(one, (queries, blocks)) * queries.shape[2] ** (-0.5)


def routed_step(embeddings, coarse_ids, fine_ids, centroids, candidates):
    wide_count = lax.axis_size("wide")
    narrow_count = lax.axis_size("narrow")
    emb_rows, width = embeddings.shape
    cent_rows = centroids.shape[0]
    group_cents = cent_rows * narrow_count
    row_cap = (2 * emb_rows + wide_count - 1) // wide_count
    exchange = functools.partial(
        lax.all_to_all, axis_name="wide", split_axis=0, concat_axis=0, tiled=True
    )
    targets = coarse_ids[:, 0]
    row_pos = targets * row_cap + slot_ranks(targets)
    send_rows = jnp.zeros((wide_count * row_cap, width), jnp.bfloat16).at[row_pos].set(embeddings)
    send_fine = jnp.full((wide_count * row_cap,), -1, jnp.int32).at[row_pos].set(fine_ids)
    flat_rows = exchange(send_rows.reshape(wide_count, row_cap, width)).reshape(-1, width)
    flat_fine = exchange(send_fine.reshape(wide_count, row_cap)).reshape(-1)
    columns = jnp.arange(group_cents, dtype=jnp.int32)
    one_hot = (flat_fine[:, None] == columns[None, :]).astype(jnp.bfloat16)
    sums = lax.psum_scatter(
        lax.dot_general(
            one_hot, flat_rows, (((0,), (0,)), ((), ())), preferred_element_type=jnp.float32
        ).astype(jnp.bfloat16),
        "narrow",
        scatter_dimension=0,
        tiled=True,
    ).astype(jnp.float32)
    mixed = centroids.astype(jnp.float32) + sums
    scale_row = lax.rsqrt(jnp.mean(mixed * mixed, axis=1, keepdims=True) + 1e-06)
    new_centroids = (mixed * scale_row).astype(jnp.bfloat16)
    gathered = lax.all_gather(new_centroids, "narrow", axis=0, tiled=True)
    block_count = group_cents // CBLK
    block_table = gathered.reshape(block_count, CBLK, width)
    query_count = emb_rows // QROWS
    requests = query_count * K_CAND
    slot_cap = (2 * requests + wide_count - 1) // wide_count
    slot_total = wide_count * slot_cap
    wanted = candidates.reshape(-1)
    owner_group = wanted // block_count
    local_block = wanted - owner_group * block_count
    req_pos = owner_group * slot_cap + slot_ranks(owner_group)
    req_query = jnp.arange(requests, dtype=jnp.int32) // K_CAND
    slot_query = jnp.zeros((slot_total,), jnp.int32).at[req_pos].set(req_query)
    slot_block = jnp.full((slot_total,), -1, jnp.int32).at[req_pos].set(local_block)
    query_blocks = embeddings.reshape(query_count, QROWS, width)
    ids_in = exchange(slot_block.reshape(wide_count, slot_cap))
    picks = jnp.clip(ids_in.reshape(-1), 0, block_count - 1)
    outgoing = pick(block_table, picks).reshape(wide_count, slot_cap, CBLK, width)
    fetched = exchange(outgoing).reshape(slot_total, CBLK, width)
    values = block_maxima(pick(query_blocks, slot_query), fetched)
    per_request = pick(values, req_pos)
    best_score = jnp.max(per_request.reshape(query_count, K_CAND, QROWS), axis=1).reshape(emb_rows)
    return (new_centroids, best_score)


def solution(mesh):
    gathered = mesh.shape["wide"] == 8 and mesh.shape["narrow"] == 4
    return jax.shard_map(
        gathered_step if gathered else routed_step,
        mesh=mesh,
        in_specs=(
            P(("wide", "narrow"), None),
            P(("wide", "narrow"), None),
            P(("wide", "narrow")),
            P(("wide", "narrow"), None),
            P(("wide", "narrow"), None),
        ),
        out_specs=(P(("wide", "narrow"), None), P(("wide", "narrow"))),
        check_vma=False,
    )
```

```python
import functools

import jax
import jax.numpy as jnp
from jax import lax
from jax.experimental import pallas as pl
from jax.experimental.pallas import tpu as pltpu
from jax.sharding import PartitionSpec as P

QROWS = 128
CBLK = 256
K_CAND = 8
WORD = 32
MESH = pl.DeviceIdType.MESH


def refine_kernel(
    emb_ref, meta_ref, cent_ref, newc_ref, best_ref,
    emb_all, meta_all, cent_all, acc, psend, precv, newc, part, part_in, load_sem,
    send_sem, recv_sem, meta_send, meta_recv, cent_sem, psum_send, psum_recv, part_send, part_recv,
):
    rows, width = emb_ref.shape
    half = rows // 2
    peers = emb_all.shape[0]
    chip_cents = cent_all.shape[0]
    tiles = chip_cents // CBLK
    wide = lax.axis_index("wide")
    narrow = lax.axis_index("narrow")
    z, x = wide // 2, wide % 2
    y, core = narrow // 2, narrow % 2
    me = wide * 2 + y
    low = z < 2
    inner = jnp.logical_or(z == 1, z == 2)
    outer = jnp.logical_not(inner)
    partner = z + 1 - 2 * (z % 2)
    across = 3 - z
    levels = (z, partner, jnp.where(low, 2, 1), jnp.where(low, 3, 0))

    def slot(column, k):
        xx = 1 - x if column in "XD" else x
        yy = 1 - y if column in "YD" else y
        return (levels[k] * 2 + xx) * 2 + yy

    slots = {c + str(k): slot(c, k) for c in "OXYD" for k in range(4)}

    def device(zz, xx, yy):
        return (zz * 2 + xx, yy * 2 + core)

    links = {
        "x": (0, device(z, 1 - x, y)),
        "y": (1, device(z, x, 1 - y)),
        "pair": (2, device(partner, x, y)),
        "cross": (3, device(across, x, y)),
    }
    twin = (wide, y * 2 + 1 - core)

    def peer(j):
        return (j // 2, (j % 2) * 2 + core)

    def chunk(link, j, h):
        number, target = links[link]
        piece = emb_all.at[j, pl.ds(h * half, half), :]
        return pltpu.make_async_remote_copy(
            src_ref=piece, dst_ref=piece, send_sem=send_sem.at[number, j, h],
            recv_sem=recv_sem.at[j, h], device_id=target, device_id_type=MESH,
        )

    sent = []

    def forward(name, h, *names):
        j = slots[name]
        for link in names:
            sent.append((link, j, h))
            if link == "cross":
                pl.when(inner)(lambda: chunk("cross", j, h).start())
            else:
                chunk(link, j, h).start()

    def forward_inner(name, h, link):
        j = slots[name]
        sent.append(("inner_" + link, j, h))
        chunk(link, j, h).start()

    def arrive(name, h):
        chunk("x", slots[name], h).wait_recv()

    def own_cents():
        return cent_all.at[pl.ds(pl.multiple_of(core * rows, rows), rows), :]

    emb_load = pltpu.make_async_copy(emb_ref, emb_all.at[me], load_sem.at[0])
    cent_load = pltpu.make_async_copy(cent_ref, own_cents(), load_sem.at[1])
    emb_load.start()
    cent_load.start()

    barrier = pltpu.get_barrier_semaphore()

    @pl.loop(1, peers)
    def _(k):
        pl.semaphore_signal(barrier, inc=1, device_id=peer((me + k) % peers), device_id_type=MESH)

    pl.semaphore_signal(barrier, inc=1, device_id=twin, device_id_type=MESH)
    meta_all[me] = meta_ref[...]
    acc[...] = jnp.zeros_like(acc)
    emb_load.wait()
    cent_load.wait()
    pl.semaphore_wait(barrier, peers)

    def meta_copy(target, source):
        return pltpu.make_async_remote_copy(
            src_ref=meta_ref, dst_ref=meta_all.at[source], send_sem=meta_send.at[target],
            recv_sem=meta_recv.at[source], device_id=peer(target), device_id_type=MESH,
        )

    cent_copy = pltpu.make_async_remote_copy(
        src_ref=own_cents(), dst_ref=own_cents(), send_sem=cent_sem.at[0],
        recv_sem=cent_sem.at[1], device_id=twin, device_id_type=MESH,
    )

    base = (wide * 4 + y * 2) * rows
    def start():
        @pl.loop(1, peers)
        def _(k):
            meta_copy((me + k) % peers, me).start()

        for h in (0, 1):
            forward("O0", h, "pair", "cross", "x")
            forward("O0", 1 - h, "y")
        cent_copy.start()

    def metas():
        @pl.loop(1, peers)
        def _(k):
            j = (me + k) % peers
            meta_copy(j, j).wait_recv()

    def corner(k):
        def go():
            arrive(f"X{k}", 0)
            forward(f"X{k}", 0, "y")
            arrive(f"Y{k}", 1)
            forward(f"Y{k}", 1, "x")

        return go

    def to_plane(name):
        def go():
            for h in (0, 1):
                forward(name, h, "x")
                forward(name, 1 - h, "y")

        return go

    def wait(name, *halves):
        def go():
            for h in halves:
                arrive(name, h)

        return go

    def wait_outer(name, *halves):
        def go():
            pl.when(outer)(wait(name, *halves))

        return go

    def to_cross(name):
        def go():
            for h in (0, 1):
                arrive(name, h)
                forward(name, h, "cross")

        return go

    def to_pair(name, *halves):
        def go():
            @pl.when(inner)
            def _():
                for h in halves:
                    arrive(name, h)
                    forward_inner(name, h, "pair")

        return go

    steps = (
        ("O0", 0, start),
        ("O0", 1),
        ("X0", 0, corner(0), metas),
        ("Y0", 1),
        ("O1", 0, to_cross("O1"), to_pair("O2", 0, 1), to_plane("O1")),
        ("O1", 1),
        ("X0", 1, wait("X0", 1)),
        ("Y0", 0, wait("Y0", 0)),
        ("D0", 0, to_cross("D0")),
        ("D0", 1),
        ("X1", 0, to_pair("O3", 0, 1), corner(1)),
        ("Y1", 1),
        ("O2", 0, wait_outer("O2", 0, 1), to_plane("O2")),
        ("O2", 1),
        ("X1", 1, wait("X1", 1)),
        ("Y1", 0, wait("Y1", 0)),
        ("D1", 0, to_pair("D2", 0, 1), to_cross("D1")),
        ("D1", 1),
        ("O3", 0, wait_outer("O3", 0, 1), to_plane("O3")),
        ("O3", 1),
        ("X2", 0, wait("X2", 0)),
        ("Y2", 1, to_pair("D3", 0), wait("Y2", 1)),
        ("X2", 1, to_pair("D3", 1), wait("X2", 1)),
        ("Y2", 0, wait("Y2", 0)),
        ("D2", 0, wait_outer("D2", 0)),
        ("D2", 1, wait_outer("D2", 1)),
        ("X3", 0, wait("X3", 0)),
        ("Y3", 1, wait("Y3", 1)),
        ("D3", 0, wait_outer("D3", 0)),
        ("X3", 1, wait("X3", 1)),
        ("Y3", 0, wait("Y3", 0)),
        ("D3", 1, wait_outer("D3", 1)),
    )

    @pl.loop(0, len(steps))
    def _(i):
        j, h = jnp.int32(0), jnp.int32(0)
        for n, (name, which, *events) in enumerate(steps):
            if events:

                @pl.when(i == n)
                def _():
                    for event in events:
                        event()

            j = j + jnp.where(i == n, slots[name], 0)
            h = h + jnp.where(i == n, which, 0)
        piece = pl.ds(pl.multiple_of(h * half, half), half)
        ids = meta_all[j, :, piece] - base
        for t in range(tiles):
            spot = lax.broadcasted_iota(jnp.int32, (CBLK, half), 0) + t * CBLK
            hot = jnp.where(spot == ids, 1.0, 0.0).astype(jnp.bfloat16)
            acc[t * CBLK : (t + 1) * CBLK, :] += jnp.dot(
                hot, emb_all[j, piece, :], preferred_element_type=jnp.float32
            )

    def psum_copy(t):
        return pltpu.make_async_remote_copy(
            src_ref=psend.at[t], dst_ref=precv.at[t], send_sem=psum_send.at[t],
            recv_sem=psum_recv.at[t], device_id=twin, device_id_type=MESH,
        )

    for t in range(tiles):
        psend[t] = acc[t * CBLK : (t + 1) * CBLK, :].astype(jnp.bfloat16)
        psum_copy(t).start()
    cent_copy.wait()

    def normalise(t):
        psum_copy(t).wait()
        mixed = cent_all[t * CBLK : (t + 1) * CBLK, :].astype(jnp.float32) + (
            psend[t].astype(jnp.float32) + precv[t].astype(jnp.float32)
        )
        scale = lax.rsqrt(jnp.mean(mixed * mixed, axis=1, keepdims=True) + 1e-06)
        newc[t * CBLK : (t + 1) * CBLK, :] = (mixed * scale).astype(jnp.bfloat16)

    def part_copy(target, source):
        return pltpu.make_async_remote_copy(
            src_ref=part.at[target], dst_ref=part_in.at[source], send_sem=part_send.at[target],
            recv_sem=part_recv.at[source], device_id=peer(target), device_id_type=MESH,
        )

    first = (wide * 4 + y * 2) * (rows // CBLK)
    word, shift = first // WORD, first % WORD

    for t in range(tiles):
        normalise(t)

    @pl.loop(1, peers + 1)
    def _(k):
        j = (me + k) % peers
        words = meta_all[j]
        bits = jnp.where(word == 0, words[:, rows : 2 * rows], words[:, 2 * rows : 3 * rows])
        best = jnp.full((1, rows), -jnp.inf, jnp.float32)
        for t in range(tiles):
            scores = lax.dot_general(
                newc[t * CBLK : (t + 1) * CBLK, :], emb_all[j], (((1,), (1,)), ((), ())),
                preferred_element_type=jnp.float32,
            )
            top = jnp.max(scores, axis=0, keepdims=True)
            live = jnp.bitwise_and(jnp.right_shift(bits, shift + t), 1) == 1
            best = jnp.maximum(best, jnp.where(live, top, -jnp.inf))
        part[j] = best

        @pl.when(k < peers)
        def _():
            part_copy(j, me).start()

    newc_ref[...] = newc[pl.ds(pl.multiple_of(core * rows, rows), rows), :]

    @pl.loop(1, peers)
    def _(k):
        j = (me + k) % peers
        part_copy(j, j).wait_recv()

    part_in[me] = part[me]
    best = part_in[0]
    for j in range(1, peers):
        best = jnp.maximum(best, part_in[j])
    best_ref[...] = best * width ** (-0.5)

    for link, j, h in sent:
        if link.startswith("inner_"):
            pl.when(inner)(lambda: chunk(link[6:], j, h).wait_send())
        elif link == "cross":
            pl.when(inner)(lambda: chunk(link, j, h).wait_send())
        else:
            chunk(link, j, h).wait_send()

    @pl.loop(1, peers)
    def _(k):
        j = (me + k) % peers
        meta_copy(j, me).wait_send()
        part_copy(j, me).wait_send()


def gathered_step(embeddings, coarse_ids, fine_ids, centroids, candidates):
    rows, width = embeddings.shape
    narrow_count = lax.axis_size("narrow")
    peers = lax.axis_size("wide") * narrow_count // 2
    assign = coarse_ids[:, 0] * (centroids.shape[0] * narrow_count) + fine_ids
    words = []
    for w in range(2):
        flags = jnp.where(
            candidates // WORD == w, jnp.left_shift(jnp.int32(1), candidates % WORD), 0
        )
        mask = flags[:, 0]
        for k in range(1, K_CAND):
            mask = jnp.bitwise_or(mask, flags[:, k])
        words.append(jnp.broadcast_to(mask[:, None], (mask.shape[0], QROWS)).reshape(rows))
    meta = jnp.concatenate([assign, *words]).reshape(1, 3 * rows)
    chip_cents = 2 * centroids.shape[0]
    tiles = chip_cents // CBLK
    new_centroids, best = pl.pallas_call(
        refine_kernel,
        out_shape=(
            jax.ShapeDtypeStruct(centroids.shape, jnp.bfloat16),
            jax.ShapeDtypeStruct((1, rows), jnp.float32),
        ),
        in_specs=[
            pl.BlockSpec(memory_space=pltpu.HBM),
            pl.BlockSpec(memory_space=pltpu.VMEM),
            pl.BlockSpec(memory_space=pltpu.HBM),
        ],
        out_specs=(pl.BlockSpec(memory_space=pltpu.VMEM),) * 2,
        scratch_shapes=[
            pltpu.VMEM((peers, rows, width), jnp.bfloat16),
            pltpu.VMEM((peers, 1, 3 * rows), jnp.int32),
            pltpu.VMEM((chip_cents, width), jnp.bfloat16),
            pltpu.VMEM((chip_cents, width), jnp.float32),
            pltpu.VMEM((tiles, CBLK, width), jnp.bfloat16),
            pltpu.VMEM((tiles, CBLK, width), jnp.bfloat16),
            pltpu.VMEM((chip_cents, width), jnp.bfloat16),
            pltpu.VMEM((peers, 1, rows), jnp.float32),
            pltpu.VMEM((peers, 1, rows), jnp.float32),
            pltpu.SemaphoreType.DMA((2,)),
            pltpu.SemaphoreType.DMA((4, peers, 2)),
            pltpu.SemaphoreType.DMA((peers, 2)),
            pltpu.SemaphoreType.DMA((peers,)),
            pltpu.SemaphoreType.DMA((peers,)),
            pltpu.SemaphoreType.DMA((2,)),
            pltpu.SemaphoreType.DMA((tiles,)),
            pltpu.SemaphoreType.DMA((tiles,)),
            pltpu.SemaphoreType.DMA((peers,)),
            pltpu.SemaphoreType.DMA((peers,)),
        ],
        compiler_params=pltpu.CompilerParams(
            collective_id=0, has_side_effects=True, vmem_limit_bytes=48 * 2**20
        ),
    )(embeddings, meta, centroids)
    return new_centroids, best.reshape(rows)


def slot_ranks(targets):
    place = jnp.arange(targets.shape[0], dtype=jnp.int32)
    same = targets[:, None] == targets[None, :]
    return jnp.sum((same & (place[None, :] < place[:, None])).astype(jnp.int32), axis=1)


def pick(table, index):
    return lax.map(lambda i: lax.dynamic_index_in_dim(table, i, keepdims=False), index)


def block_maxima(queries, blocks):
    def one(operands):
        query, block = operands
        scores = jnp.einsum("nd,cd->nc", query, block, preferred_element_type=jnp.float32)
        return jnp.max(scores, axis=1)

    return lax.map(one, (queries, blocks)) * queries.shape[2] ** (-0.5)


def routed_step(embeddings, coarse_ids, fine_ids, centroids, candidates):
    wide_count = lax.axis_size("wide")
    narrow_count = lax.axis_size("narrow")
    emb_rows, width = embeddings.shape
    cent_rows = centroids.shape[0]
    group_cents = cent_rows * narrow_count
    row_cap = (2 * emb_rows + wide_count - 1) // wide_count
    exchange = functools.partial(
        lax.all_to_all, axis_name="wide", split_axis=0, concat_axis=0, tiled=True
    )
    targets = coarse_ids[:, 0]
    row_pos = targets * row_cap + slot_ranks(targets)
    send_rows = jnp.zeros((wide_count * row_cap, width), jnp.bfloat16).at[row_pos].set(embeddings)
    send_fine = jnp.full((wide_count * row_cap,), -1, jnp.int32).at[row_pos].set(fine_ids)
    flat_rows = exchange(send_rows.reshape(wide_count, row_cap, width)).reshape(-1, width)
    flat_fine = exchange(send_fine.reshape(wide_count, row_cap)).reshape(-1)
    columns = jnp.arange(group_cents, dtype=jnp.int32)
    one_hot = (flat_fine[:, None] == columns[None, :]).astype(jnp.bfloat16)
    sums = lax.psum_scatter(
        lax.dot_general(
            one_hot, flat_rows, (((0,), (0,)), ((), ())), preferred_element_type=jnp.float32
        ).astype(jnp.bfloat16),
        "narrow",
        scatter_dimension=0,
        tiled=True,
    ).astype(jnp.float32)
    mixed = centroids.astype(jnp.float32) + sums
    scale_row = lax.rsqrt(jnp.mean(mixed * mixed, axis=1, keepdims=True) + 1e-06)
    new_centroids = (mixed * scale_row).astype(jnp.bfloat16)
    gathered = lax.all_gather(new_centroids, "narrow", axis=0, tiled=True)
    block_count = group_cents // CBLK
    block_table = gathered.reshape(block_count, CBLK, width)
    query_count = emb_rows // QROWS
    requests = query_count * K_CAND
    slot_cap = (2 * requests + wide_count - 1) // wide_count
    slot_total = wide_count * slot_cap
    wanted = candidates.reshape(-1)
    owner_group = wanted // block_count
    local_block = wanted - owner_group * block_count
    req_pos = owner_group * slot_cap + slot_ranks(owner_group)
    req_query = jnp.arange(requests, dtype=jnp.int32) // K_CAND
    slot_query = jnp.zeros((slot_total,), jnp.int32).at[req_pos].set(req_query)
    slot_block = jnp.full((slot_total,), -1, jnp.int32).at[req_pos].set(local_block)
    query_blocks = embeddings.reshape(query_count, QROWS, width)
    ids_in = exchange(slot_block.reshape(wide_count, slot_cap))
    picks = jnp.clip(ids_in.reshape(-1), 0, block_count - 1)
    outgoing = pick(block_table, picks).reshape(wide_count, slot_cap, CBLK, width)
    fetched = exchange(outgoing).reshape(slot_total, CBLK, width)
    values = block_maxima(pick(query_blocks, slot_query), fetched)
    per_request = pick(values, req_pos)
    best_score = jnp.max(per_request.reshape(query_count, K_CAND, QROWS), axis=1).reshape(emb_rows)
    return (new_centroids, best_score)


def solution(mesh):
    gathered = mesh.shape["wide"] == 8 and mesh.shape["narrow"] == 4
    return jax.shard_map(
        gathered_step if gathered else routed_step,
        mesh=mesh,
        in_specs=(
            P(("wide", "narrow"), None),
            P(("wide", "narrow"), None),
            P(("wide", "narrow")),
            P(("wide", "narrow"), None),
            P(("wide", "narrow"), None),
        ),
        out_specs=(P(("wide", "narrow"), None), P(("wide", "narrow"))),
        check_vma=False,
    )
```
